32 devices in a mesh: row: 4 (over z), col: 8 (over y, x, core).
Axes of the slice: x: 2, y: 2, z: 4, core: 2. Of those that a mesh axis runs over, the one named last changes fastest.
Arguments:
- matrix_real: bfloat16 [128, 16384], P('col', 'row'), may hold values from -0.5 to 0.5
- matrix_imag: bfloat16 [128, 16384], P('col', 'row'), may hold values from -0.5 to 0.5
- valence_index: int32 [128], P('col'), may hold values from 0 to 15
- conduction_index: int32 [128], P('col'), may hold values from 0 to 31
- valence_energy: float32 [16], replicated, may hold values from -1.5 to -0.1
- conduction_energy: float32 [32], replicated, may hold values from 0.1 to 2
- frequency: float32 [2], replicated, may hold values from 0.2 to 2
Outputs:
- chi_real: bfloat16 [2, 16384, 16384], P(None, 'row', 'col')
- chi_imag: bfloat16 [2, 16384, 16384], P(None, 'row', 'col')
The draws below stay inside these ranges and needn't reach their ends.
All inputs are finite; a program needn't handle non-finite values.
Results may differ from the reference program's by a relative error of at most 0.005.
Values may be sent and summed in bfloat16 or wider, within the bound.
A program may use at most 384 MiB of HBM per device.

```python
import math
import jax
import jax.numpy as jnp

NG = 16384
NF = 2
NV = 16
NC = 32
NP = 128


def place_ends(entries, own_key, least, high):
    dims = entries.shape
    place = [jax.random.randint(jax.random.fold_in(own_key, axis), (), 0, dims[axis]) for axis in range(len(dims))]
    entries = entries.at[tuple(place)].set(least)
    longest = dims.index(max(dims))
    place[longest] = (place[longest] + 1) % dims[longest]
    return entries.at[tuple(place)].set(high)


def block_scale(stream_key, shape, split, low, high):
    loudness, own = 1.0, jax.random.fold_in(stream_key, 6)
    for position, blocks in split:
        steps = jnp.exp(jax.random.uniform(jax.random.fold_in(own, position), (blocks,), jnp.float32, low / len(split), high / len(split)))
        loudness = loudness * jnp.repeat(steps, shape[position] // blocks).reshape([-1 if axis == position else 1 for axis in range(len(shape))])
    return loudness


def gaussian(rng, extent, width, reach, pieces=(), dtype=jnp.bfloat16):
    array = jax.random.normal(rng, extent, jnp.float32) * width
    if len(pieces) > 0:
        array = block_scale(rng, extent, pieces, -0.22, 0.18) * array
    return jnp.clip(array, min=-reach, max=reach).astype(dtype)


def setup_inputs(seed: int = 0) -> dict:
    arg_keys = jax.random.split(jax.random.key(seed), 8)
    matrix_real = gaussian(arg_keys[0], (NP, NG), NP ** -0.5, 0.5, ((0, 8), (1, 4)))
    matrix_imag = gaussian(arg_keys[1], (NP, NG), NP ** -0.5, 0.5, ((0, 8), (1, 4)))
    valence_index = place_ends(jax.random.randint(arg_keys[2], (NP,), 0, NV), jax.random.fold_in(arg_keys[2], 1), 0, NV - 1).astype(jnp.int32)
    conduction_index = place_ends(jax.random.randint(arg_keys[3], (NP,), 0, NC), jax.random.fold_in(arg_keys[3], 1), 0, NC - 1).astype(jnp.int32)
    valence_energy = jnp.clip(jax.random.uniform(arg_keys[4], (NV,), jnp.float32, -1.5, -0.1), -1.5, -0.1)
    conduction_energy = jnp.clip(jax.random.uniform(arg_keys[5], (NC,), jnp.float32, 0.1, 2.0), 0.1, 2.0)
    frequency = jnp.clip(jnp.exp(jax.random.uniform(arg_keys[6], (NF,), jnp.float32, math.log(0.2), math.log(2.0))), 0.2, 2.0)
    return {"matrix_real": matrix_real, "matrix_imag": matrix_imag, "valence_index": valence_index, "conduction_index": conduction_index, "valence_energy": valence_energy, "conduction_energy": conduction_energy, "frequency": frequency}


def reference(matrix_real, matrix_imag, valence_index, conduction_index, valence_energy, conduction_energy, frequency):
    gap = conduction_energy[conduction_index] - valence_energy[valence_index]
    real_out = []
    imag_out = []
    for index in range(NF):
        omega = frequency[index]
        weight = 4.0 * gap / (gap * gap + omega * omega)
        scaled_real = (weight[:, None] * matrix_real.astype(jnp.float32)).astype(jnp.bfloat16)
        scaled_imag = (weight[:, None] * matrix_imag.astype(jnp.float32)).astype(jnp.bfloat16)
        chi_real = jnp.dot(matrix_real.T, scaled_real, preferred_element_type=jnp.float32)
        chi_real = -(chi_real + jnp.dot(matrix_imag.T, scaled_imag, preferred_element_type=jnp.float32))
        chi_imag = jnp.dot(matrix_real.T, scaled_imag, preferred_element_type=jnp.float32)
        chi_imag = -(chi_imag - jnp.dot(matrix_imag.T, scaled_real, preferred_element_type=jnp.float32))
        real_out.append(chi_real.astype(jnp.bfloat16))
        imag_out.append(chi_imag.astype(jnp.bfloat16))
    return jnp.stack(real_out, axis=0), jnp.stack(imag_out, axis=0)
```

```python
import functools

import jax
import jax.numpy as jnp
from jax import lax
from jax.experimental import pallas as pl
from jax.experimental.pallas import tpu as pltpu
from jax.sharding import PartitionSpec as P

MESH = pl.DeviceIdType.MESH
ANY = pl.BlockSpec(memory_space=pl.ANY)
SMEM = pl.BlockSpec(memory_space=pltpu.SMEM)
VMEM = pl.BlockSpec(memory_space=pltpu.VMEM)


def flip(index, mask):
    result = index
    bit = 1
    while bit <= mask:
        if mask & bit:
            result = result + bit * (1 - 2 * ((index // bit) % 2))
        bit *= 2
    return result


def chain_order(cols):
    order = [0, 1]
    evens = list(range(2, cols, 2))
    for even in evens:
        order.append(even)
    for even in evens:
        order.append(even + 1)
    return order


def gather_kernel(
    rows,
    cols,
    real_ref,
    imag_ref,
    valence_ref,
    conduction_ref,
    valence_energy_ref,
    conduction_energy_ref,
    left_ref,
    right_ref,
    gap_ref,
    left_send,
    left_forward,
    left_recv,
    up_send,
    down_send,
    right_recv,
    gap_send,
    gap_recv,
    local_sem,
):
    z = lax.axis_index("row")
    j = lax.axis_index("col")
    pairs = real_ref.shape[0]
    width = right_ref.shape[2]
    per_plane = cols // rows
    home = j // per_plane
    offset = pl.multiple_of((j % per_plane) * width, width)
    sibling = flip(j, 1)
    is_source = z == home
    sends_up = (z >= home) & (z < rows - 1)
    sends_down = (z <= home) & (z > 0)

    barrier = pltpu.get_barrier_semaphore()
    for step in range(1, cols):
        pl.semaphore_signal(
            barrier, inc=1, device_id=(z, flip(j, step)), device_id_type=MESH
        )

    @pl.when(z > 0)
    def _():
        pl.semaphore_signal(barrier, inc=1, device_id=(z - 1, j), device_id_type=MESH)

    @pl.when(z < rows - 1)
    def _():
        pl.semaphore_signal(barrier, inc=1, device_id=(z + 1, j), device_id_type=MESH)

    ends = jnp.where((z == 0) | (z == rows - 1), 1, 2)
    pl.semaphore_wait(barrier, cols - 1 + ends)

    def remote(src, dst, send_sem, recv_sem, device):
        return pltpu.make_async_remote_copy(
            src_ref=src,
            dst_ref=dst,
            send_sem=send_sem,
            recv_sem=recv_sem,
            device_id=device,
            device_id_type=MESH,
        )

    halves = ((real_ref, 0), (imag_ref, pairs))
    directions = ((sends_up, up_send, 1), (sends_down, down_send, -1))

    for sends, send_sem, hop in directions:

        @pl.when(sends & is_source)
        def _(send_sem=send_sem, hop=hop):
            for ref, start in halves:
                remote(
                    ref.at[:, pl.ds(offset, width)],
                    right_ref.at[j, pl.ds(start, pairs), :],
                    send_sem.at[0],
                    right_recv.at[0],
                    (z + hop, j),
                ).start()

    for step in list(range(2, cols, 2)) + [1]:
        for ref, start in halves:
            remote(
                ref,
                left_ref.at[j, pl.ds(start, pairs), :],
                left_send.at[step],
                left_recv.at[step],
                (z, flip(j, step)),
            ).start()

    for ref, start in halves:
        pltpu.make_async_copy(
            ref, left_ref.at[j, pl.ds(start, pairs), :], local_sem.at[0]
        ).start()

    for pair in range(pairs):
        gap = (
            conduction_energy_ref[conduction_ref[pair]]
            - valence_energy_ref[valence_ref[pair]]
        )
        gap_ref[j, pair : pair + 1, :] = jnp.full((1, gap_ref.shape[2]), gap)
    for step in range(1, cols):
        remote(
            gap_ref.at[j],
            gap_ref.at[j],
            gap_send.at[step],
            gap_recv.at[step],
            (z, flip(j, step)),
        ).start()

    def left_wait(step):
        shard = flip(j, step)
        if step == 0:
            pltpu.make_async_copy(
                left_ref.at[shard], left_ref.at[shard], local_sem.at[0]
            ).wait()
        else:
            remote(
                left_ref.at[shard],
                left_ref.at[shard],
                left_send.at[step],
                left_recv.at[step],
                (z, sibling),
            ).wait_recv()

    def hand_on(src, step, sends, send_sem, hop):
        shard = flip(j, step)

        @pl.when(sends)
        def _():
            remote(
                src,
                right_ref.at[shard],
                send_sem.at[step],
                right_recv.at[step],
                (z + hop, j),
            ).start()

    def left_step(step):
        shard = flip(j, step)
        left_wait(step)
        part = left_ref.at[shard, :, pl.ds(offset, width)]
        if step > 0:
            for sends, send_sem, hop in directions:
                hand_on(part, step, sends & is_source, send_sem, hop)
        if step % 2 == 0 and step > 0:
            remote(
                left_ref.at[shard],
                left_ref.at[shard],
                left_forward.at[step],
                left_recv.at[step + 1],
                (z, sibling),
            ).start()

        @pl.when(is_source)
        def _():
            pltpu.make_async_copy(
                part, right_ref.at[shard], right_recv.at[step]
            ).start()

    def right_wait(step):
        shard = flip(j, step)
        pltpu.make_async_copy(
            right_ref.at[shard], right_ref.at[shard], right_recv.at[step]
        ).wait()

    def right_step(step):
        @pl.when(jnp.logical_not(is_source))
        def _():
            right_wait(step)
            for sends, send_sem, hop in directions:
                hand_on(right_ref.at[flip(j, step)], step, sends, send_sem, hop)

    order = chain_order(cols)
    behind = 2
    for position in range(len(order) + behind):
        if position < len(order):
            left_step(order[position])
        if position >= behind:
            right_step(order[position - behind])

    @pl.when(is_source)
    def _():
        for step in range(cols):
            right_wait(step)

    for step in range(1, cols):
        remote(
            gap_ref.at[j], gap_ref.at[flip(j, step)], gap_send.at[step],
            gap_recv.at[step], (z, sibling),
        ).wait()

    def sent(shard_ref, sem):
        remote(shard_ref, shard_ref, sem, left_recv.at[0], (z, sibling)).wait_send()

    for step in range(1, cols):
        if step == 1 or step % 2 == 0:
            sent(left_ref.at[j], left_send.at[step])
        if step % 2 == 0:
            sent(left_ref.at[j], left_forward.at[step])
    for sends, send_sem, hop in directions:

        @pl.when(sends)
        def _(send_sem=send_sem):
            for step in range(cols):
                sent(right_ref.at[j], send_sem.at[step])


def gather(rows, cols, width, matrix_real, matrix_imag, indices):
    pairs, depth = matrix_real.shape
    dma = pltpu.SemaphoreType.DMA((cols,))
    return pl.pallas_call(
        functools.partial(gather_kernel, rows, cols),
        out_shape=(
            jax.ShapeDtypeStruct((cols, 2 * pairs, depth), jnp.bfloat16),
            jax.ShapeDtypeStruct((cols, 2 * pairs, width), jnp.bfloat16),
            jax.ShapeDtypeStruct((cols, pairs, 128), jnp.float32),
        ),
        in_specs=[ANY, ANY, SMEM, SMEM, SMEM, SMEM],
        out_specs=(ANY, ANY, VMEM),
        scratch_shapes=[dma] * 9,
        compiler_params=pltpu.CompilerParams(collective_id=0, has_side_effects=True),
    )(matrix_real, matrix_imag, *indices)


def product_kernel(
    count, pairs, frequency_ref, gap_ref, right_ref, left_ref, real_ref, imag_ref, scaled
):
    cols, both, width = right_ref.shape

    @pl.when(pl.program_id(0) == 0)
    def _():
        def shard_scale(shard, carry):
            gap = gap_ref[shard]
            base = pl.multiple_of(shard * both, both)
            wide_real = right_ref[shard, :pairs, :].astype(jnp.float32)
            wide_imag = right_ref[shard, pairs:, :].astype(jnp.float32)
            for index in range(count):
                omega = frequency_ref[index]
                weight = (4.0 * gap / (gap * gap + omega * omega))[:, :1]
                scaled_real = (weight * wide_real).astype(jnp.bfloat16)
                scaled_imag = (weight * wide_imag).astype(jnp.bfloat16)
                upper = pl.ds(base, pairs)
                lower = pl.ds(base + pairs, pairs)
                scaled[2 * index, upper, :] = -scaled_real
                scaled[2 * index, lower, :] = -scaled_imag
                scaled[2 * index + 1, upper, :] = -scaled_imag
                scaled[2 * index + 1, lower, :] = scaled_real
            return carry

        lax.fori_loop(0, cols, shard_scale, 0)

    left = left_ref[...].reshape(cols * both, left_ref.shape[2])
    left = left.T
    chunk = min(width, 512)
    for index in range(count):
        for part, out_ref in ((0, real_ref), (1, imag_ref)):
            for start in range(0, width, chunk):
                out_ref[index, :, start : start + chunk] = jnp.dot(
                    left,
                    scaled[2 * index + part, :, start : start + chunk],
                    preferred_element_type=jnp.float32,
                ).astype(out_ref.dtype)


def product(frequency, gap, right, left):
    cols, both, depth = left.shape
    width = right.shape[2]
    count = frequency.shape[0]
    tile = 256
    out = jax.ShapeDtypeStruct((count, depth, width), jnp.bfloat16)
    out_spec = pl.BlockSpec((count, tile, width), lambda i: (0, i, 0))
    return pl.pallas_call(
        functools.partial(product_kernel, count, both // 2),
        out_shape=(out, out),
        grid=(depth // tile,),
        in_specs=[
            SMEM,
            pl.BlockSpec(gap.shape, lambda i: (0, 0, 0)),
            pl.BlockSpec(right.shape, lambda i: (0, 0, 0)),
            pl.BlockSpec((cols, both, tile), lambda i: (0, 0, i)),
        ],
        out_specs=(out_spec, out_spec),
        scratch_shapes=[pltpu.VMEM((2 * count, cols * both, width), jnp.bfloat16)],
        compiler_params=pltpu.CompilerParams(vmem_limit_bytes=48 * 1024 * 1024),
    )(frequency, gap, right, left)


def solution(mesh):
    rows, cols = mesh.shape["row"], mesh.shape["col"]

    def on_device(matrix_real, matrix_imag, valence_index, conduction_index,
                  valence_energy, conduction_energy, frequency):
        width = matrix_real.shape[1] * rows // cols
        left, right, gap = gather(
            rows, cols, width, matrix_real, matrix_imag,
            (valence_index, conduction_index, valence_energy, conduction_energy),
        )
        return product(frequency, gap, right, left)

    placed = (P("col", "row"), P("col", "row"), P("col"), P("col"), P(), P(), P())
    return jax.shard_map(
        on_device,
        mesh=mesh,
        in_specs=placed,
        out_specs=(P(None, "row", "col"), P(None, "row", "col")),
        check_vma=False,
    )
```

```python
import functools

import jax
import jax.numpy as jnp
from jax import lax
from jax.experimental import pallas as pl
from jax.experimental.pallas import tpu as pltpu
from jax.sharding import PartitionSpec as P

MESH = pl.DeviceIdType.MESH
SMEM = pl.BlockSpec(memory_space=pltpu.SMEM)
VMEM = pl.BlockSpec(memory_space=pltpu.VMEM)


def flip(index, mask):
    result = index
    bit = 1
    while bit <= mask:
        if mask & bit:
            result = result + bit * (1 - 2 * ((index // bit) % 2))
        bit *= 2
    return result


def chain_order(cols):
    order = [0, 1]
    evens = list(range(2, cols, 2))
    for even in evens:
        order.append(even)
    for even in evens:
        order.append(even + 1)
    return order


def gather_kernel(
    rows,
    cols,
    real_ref,
    imag_ref,
    valence_ref,
    conduction_ref,
    valence_energy_ref,
    conduction_energy_ref,
    left_ref,
    right_ref,
    gap_ref,
    left_send,
    left_forward,
    left_recv,
    up_send,
    down_send,
    right_recv,
    gap_send,
    gap_recv,
):
    z = lax.axis_index("row")
    j = lax.axis_index("col")
    pairs = real_ref.shape[0]
    width = right_ref.shape[2]
    per_plane = cols // rows
    home = j // per_plane
    offset = pl.multiple_of((j % per_plane) * width, width)
    sibling = flip(j, 1)
    is_source = z == home
    sends_up = (z >= home) & (z < rows - 1)
    sends_down = (z <= home) & (z > 0)

    barrier = pltpu.get_barrier_semaphore()
    for step in range(1, cols):
        pl.semaphore_signal(
            barrier, inc=1, device_id=(z, flip(j, step)), device_id_type=MESH
        )

    @pl.when(z > 0)
    def _():
        pl.semaphore_signal(barrier, inc=1, device_id=(z - 1, j), device_id_type=MESH)

    @pl.when(z < rows - 1)
    def _():
        pl.semaphore_signal(barrier, inc=1, device_id=(z + 1, j), device_id_type=MESH)

    ends = jnp.where((z == 0) | (z == rows - 1), 1, 2)
    pl.semaphore_wait(barrier, cols - 1 + ends)

    def remote(src, dst, send_sem, recv_sem, device):
        return pltpu.make_async_remote_copy(
            src_ref=src,
            dst_ref=dst,
            send_sem=send_sem,
            recv_sem=recv_sem,
            device_id=device,
            device_id_type=MESH,
        )

    directions = ((sends_up, up_send, 1), (sends_down, down_send, -1))
    strip = pl.ds(offset, width)

    left_ref[j, :pairs, :] = real_ref[...]
    left_ref[j, pairs:, :] = imag_ref[...]

    def hand_on(src, step, sends, send_sem, hop):
        @pl.when(sends)
        def _():
            remote(
                src,
                right_ref.at[flip(j, step)],
                send_sem.at[step],
                right_recv.at[step],
                (z + hop, j),
            ).start()

    for sends, send_sem, hop in directions:
        hand_on(left_ref.at[j, :, strip], 0, sends & is_source, send_sem, hop)
    for step in list(range(2, cols, 2)) + [1]:
        remote(
            left_ref.at[j],
            left_ref.at[j],
            left_send.at[step],
            left_recv.at[step],
            (z, flip(j, step)),
        ).start()

    for pair in range(pairs):
        gap = (
            conduction_energy_ref[conduction_ref[pair]]
            - valence_energy_ref[valence_ref[pair]]
        )
        gap_ref[j, pair : pair + 1, :] = jnp.full((1, gap_ref.shape[2]), gap)
    for step in range(1, cols):
        remote(
            gap_ref.at[j],
            gap_ref.at[j],
            gap_send.at[step],
            gap_recv.at[step],
            (z, flip(j, step)),
        ).start()

    def left_step(step):
        shard = flip(j, step)
        if step > 0:
            remote(
                left_ref.at[shard],
                left_ref.at[shard],
                left_send.at[step],
                left_recv.at[step],
                (z, sibling),
            ).wait_recv()
            for sends, send_sem, hop in directions:
                hand_on(
                    left_ref.at[shard, :, strip], step, sends & is_source, send_sem, hop
                )
        if step % 2 == 0 and step > 0:
            remote(
                left_ref.at[shard],
                left_ref.at[shard],
                left_forward.at[step],
                left_recv.at[step + 1],
                (z, sibling),
            ).start()

        @pl.when(is_source)
        def _():
            right_ref[shard] = left_ref[shard, :, strip]

    def right_wait(step):
        shard = flip(j, step)
        pltpu.make_async_copy(
            right_ref.at[shard], right_ref.at[shard], right_recv.at[step]
        ).wait()

    def right_step(step):
        @pl.when(jnp.logical_not(is_source))
        def _():
            right_wait(step)
            for sends, send_sem, hop in directions:
                hand_on(right_ref.at[flip(j, step)], step, sends, send_sem, hop)

    order = chain_order(cols)
    behind = 2
    for position in range(len(order) + behind):
        if position < len(order):
            left_step(order[position])
        if position >= behind:
            right_step(order[position - behind])

    for step in range(1, cols):
        remote(
            gap_ref.at[j], gap_ref.at[flip(j, step)], gap_send.at[step],
            gap_recv.at[step], (z, sibling),
        ).wait()

    def sent(shard_ref, sem):
        remote(shard_ref, shard_ref, sem, left_recv.at[0], (z, sibling)).wait_send()

    for step in range(1, cols):
        if step == 1 or step % 2 == 0:
            sent(left_ref.at[j], left_send.at[step])
        if step % 2 == 0:
            sent(left_ref.at[j], left_forward.at[step])
    for sends, send_sem, hop in directions:

        @pl.when(sends)
        def _(send_sem=send_sem):
            for step in range(cols):
                sent(right_ref.at[j], send_sem.at[step])


def gather(rows, cols, width, matrix_real, matrix_imag, indices):
    pairs, depth = matrix_real.shape
    dma = pltpu.SemaphoreType.DMA((cols,))
    return pl.pallas_call(
        functools.partial(gather_kernel, rows, cols),
        out_shape=(
            jax.ShapeDtypeStruct((cols, 2 * pairs, depth), jnp.bfloat16),
            jax.ShapeDtypeStruct((cols, 2 * pairs, width), jnp.bfloat16),
            jax.ShapeDtypeStruct((cols, pairs, 128), jnp.float32),
        ),
        in_specs=[VMEM, VMEM, SMEM, SMEM, SMEM, SMEM],
        out_specs=(VMEM, VMEM, VMEM),
        scratch_shapes=[dma] * 8,
        compiler_params=pltpu.CompilerParams(
            collective_id=0, has_side_effects=True, vmem_limit_bytes=60 * 1024 * 1024
        ),
    )(matrix_real, matrix_imag, *indices)


def product_kernel(
    count, pairs, frequency_ref, gap_ref, right_ref, left_ref, real_ref, imag_ref, scaled, turned
):
    cols, both, width = right_ref.shape

    index = pl.program_id(1)
    start = pl.program_id(2)

    @pl.when((pl.program_id(0) == 0) & (index == 0) & (start == 0))
    def _():
        def shard_scale(shard, carry):
            gap = gap_ref[shard]
            base = pl.multiple_of(shard * both, both)
            wide_real = right_ref[shard, :pairs, :].astype(jnp.float32)
            wide_imag = right_ref[shard, pairs:, :].astype(jnp.float32)
            for index in range(count):
                omega = frequency_ref[index]
                weight = (4.0 * gap / (gap * gap + omega * omega))[:, :1]
                scaled_real = (weight * wide_real).astype(jnp.bfloat16)
                scaled_imag = (weight * wide_imag).astype(jnp.bfloat16)
                upper = pl.ds(base, pairs)
                lower = pl.ds(base + pairs, pairs)
                scaled[2 * index, upper, :] = -scaled_real
                scaled[2 * index, lower, :] = -scaled_imag
                scaled[2 * index + 1, upper, :] = -scaled_imag
                scaled[2 * index + 1, lower, :] = scaled_real
            return carry

        lax.fori_loop(0, cols, shard_scale, 0)

    @pl.when((index == 0) & (start == 0))
    def _():
        turned[...] = left_ref[...].reshape(cols * both, left_ref.shape[2]).T

    block = real_ref.shape[2]
    chunk = 256
    for part, out_ref in ((0, real_ref), (1, imag_ref)):
        for place in range(0, block, chunk):
            columns = pl.ds(pl.multiple_of(start * block + place, chunk), chunk)
            out_ref[0, :, place : place + chunk] = jnp.dot(
                turned[...],
                scaled[2 * index + part, :, columns],
                preferred_element_type=jnp.float32,
            ).astype(out_ref.dtype)


def product(frequency, gap, right, left):
    cols, both, depth = left.shape
    width = right.shape[2]
    count = frequency.shape[0]
    tile = 1024
    block = min(width, 1024)
    out = jax.ShapeDtypeStruct((count, depth, width), jnp.bfloat16)
    out_spec = pl.BlockSpec((1, tile, block), lambda i, f, h: (f, i, h))
    return pl.pallas_call(
        functools.partial(product_kernel, count, both // 2),
        out_shape=(out, out),
        grid=(depth // tile, count, width // block),
        in_specs=[
            SMEM,
            pl.BlockSpec(gap.shape, lambda i, f, h: (0, 0, 0)),
            pl.BlockSpec(right.shape, lambda i, f, h: (0, 0, 0)),
            pl.BlockSpec((cols, both, tile), lambda i, f, h: (0, 0, i)),
        ],
        out_specs=(out_spec, out_spec),
        scratch_shapes=[
            pltpu.VMEM((2 * count, cols * both, width), jnp.bfloat16),
            pltpu.VMEM((tile, cols * both), jnp.bfloat16),
        ],
        compiler_params=pltpu.CompilerParams(vmem_limit_bytes=60 * 1024 * 1024),
    )(frequency, gap, right, left)


def solution(mesh):
    rows, cols = mesh.shape["row"], mesh.shape["col"]

    def on_device(matrix_real, matrix_imag, valence_index, conduction_index,
                  valence_energy, conduction_energy, frequency):
        width = matrix_real.shape[1] * rows // cols
        left, right, gap = gather(
            rows, cols, width, matrix_real, matrix_imag,
            (valence_index, conduction_index, valence_energy, conduction_energy),
        )
        return product(frequency, gap, right, left)

    placed = (P("col", "row"), P("col", "row"), P("col"), P("col"), P(), P(), P())
    return jax.shard_map(
        on_device,
        mesh=mesh,
        in_specs=placed,
        out_specs=(P(None, "row", "col"), P(None, "row", "col")),
        check_vma=False,
    )
```

```python
import functools

import jax
import jax.numpy as jnp
from jax import lax
from jax.experimental import pallas as pl
from jax.experimental.pallas import tpu as pltpu
from jax.sharding import PartitionSpec as P

MESH = pl.DeviceIdType.MESH
SMEM = pl.BlockSpec(memory_space=pltpu.SMEM)
VMEM = pl.BlockSpec(memory_space=pltpu.VMEM)


def flip(index, mask):
    result = index
    bit = 1
    while bit <= mask:
        if mask & bit:
            result = result + bit * (1 - 2 * ((index // bit) % 2))
        bit *= 2
    return result


def gather_kernel(
    rows,
    cols,
    real_ref,
    imag_ref,
    valence_ref,
    conduction_ref,
    valence_energy_ref,
    conduction_energy_ref,
    turned_ref,
    right_ref,
    gap_ref,
    left_ref,
    line_ref,
    left_send,
    left_forward,
    left_recv,
    up_send,
    down_send,
    line_recv,
    right_send,
    right_recv,
    gap_send,
    gap_recv,
):
    z = lax.axis_index("row")
    j = lax.axis_index("col")
    pairs, depth = real_ref.shape
    width = right_ref.shape[2]
    per_plane = cols // rows
    home = j // per_plane
    sibling = flip(j, 1)

    barrier = pltpu.get_barrier_semaphore()
    for step in range(1, cols):
        pl.semaphore_signal(
            barrier, inc=1, device_id=(z, flip(j, step)), device_id_type=MESH
        )

    @pl.when(z > 0)
    def _():
        pl.semaphore_signal(barrier, inc=1, device_id=(z - 1, j), device_id_type=MESH)

    @pl.when(z < rows - 1)
    def _():
        pl.semaphore_signal(barrier, inc=1, device_id=(z + 1, j), device_id_type=MESH)

    line_ref[z, :pairs, :] = real_ref[...]
    line_ref[z, pairs:, :] = imag_ref[...]
    left_ref[j, :pairs, :] = real_ref[...]
    left_ref[j, pairs:, :] = imag_ref[...]

    ends = jnp.where((z == 0) | (z == rows - 1), 1, 2)
    pl.semaphore_wait(barrier, cols - 1 + ends)

    def remote(src, dst, send_sem, recv_sem, device):
        return pltpu.make_async_remote_copy(
            src_ref=src,
            dst_ref=dst,
            send_sem=send_sem,
            recv_sem=recv_sem,
            device_id=device,
            device_id_type=MESH,
        )

    def hand_on(plane, strip, send_sem, hop, allowed):
        part = line_ref.at[plane, :, strip * width : (strip + 1) * width]
        slot = plane * per_plane + strip

        @pl.when(allowed)
        def _():
            remote(
                part, part, send_sem.at[slot], line_recv.at[slot], (z + hop, j)
            ).start()

    for strip in range(per_plane):
        hand_on(z, strip, up_send, 1, z < rows - 1)
        hand_on(z, strip, down_send, -1, z > 0)
    for step in list(range(2, cols, 2)) + [1]:
        remote(
            left_ref.at[j],
            left_ref.at[j],
            left_send.at[step],
            left_recv.at[step],
            (z, flip(j, step)),
        ).start()

    for pair in range(pairs):
        gap = (
            conduction_energy_ref[conduction_ref[pair]]
            - valence_energy_ref[valence_ref[pair]]
        )
        gap_ref[j, pair : pair + 1, :] = jnp.full((1, gap_ref.shape[2]), gap)
    for step in range(1, cols):
        remote(
            gap_ref.at[j],
            gap_ref.at[j],
            gap_send.at[step],
            gap_recv.at[step],
            (z, flip(j, step)),
        ).start()

    def line_step(distance):
        for strip in range(per_plane):
            for hop, send_sem in ((1, up_send), (-1, down_send)):
                plane = z - hop * distance

                @pl.when((plane >= 0) & (plane < rows))
                def _(strip=strip, hop=hop, send_sem=send_sem, plane=plane):
                    slot = plane * per_plane + strip
                    lanes = slice(strip * width, (strip + 1) * width)
                    part = line_ref.at[plane, :, lanes]
                    remote(
                        part, part, send_sem.at[slot], line_recv.at[slot], (z, sibling)
                    ).wait_recv()
                    hand_on(
                        plane, strip, send_sem, hop, (z + hop >= 0) & (z + hop < rows)
                    )

                    @pl.when(slot == j)
                    def _():
                        right_ref[j] = line_ref[plane, :, lanes]

                    @pl.when(slot != j)
                    def _():
                        remote(
                            part,
                            right_ref.at[j],
                            right_send.at[slot],
                            right_recv.at[j],
                            (z, slot),
                        ).start()

    def left_wait(step):
        shard = flip(j, step)
        part = left_ref.at[shard]
        remote(
            part, part, left_send.at[step], left_recv.at[step], (z, sibling)
        ).wait_recv()
        if step % 2 == 0:
            remote(
                part,
                part,
                left_forward.at[step],
                left_recv.at[step + 1],
                (z, sibling),
            ).start()

    for distance in range(1, rows - 1):
        line_step(distance)
    for step in range(2, cols, 2):
        left_wait(step)
    line_step(rows - 1)
    for step in range(1, cols, 2):
        left_wait(step)

    tile = 512

    def turn(index, carry):
        lanes = pl.ds(pl.multiple_of(index * tile, tile), tile)
        block = left_ref[:, :, lanes].reshape(cols * 2 * pairs, tile)
        turned_ref[lanes, :] = block.T
        return carry

    lax.fori_loop(0, depth // tile, turn, 0)

    @pl.when(z == home)
    def _():
        lanes = pl.ds(pl.multiple_of((j % per_plane) * width, width), width)
        for shard in range(cols):
            right_ref[shard] = left_ref[shard, :, lanes]

    @pl.when(z != home)
    def _():
        for step in range(1, cols):
            shard = flip(j, step)
            remote(
                right_ref.at[shard],
                right_ref.at[shard],
                right_send.at[0],
                right_recv.at[shard],
                (z, sibling),
            ).wait_recv()

    for step in range(1, cols):
        remote(
            gap_ref.at[j], gap_ref.at[flip(j, step)], gap_send.at[step],
            gap_recv.at[step], (z, sibling),
        ).wait()

    def sent(shard_ref, sem):
        remote(shard_ref, shard_ref, sem, left_recv.at[0], (z, sibling)).wait_send()

    for step in range(1, cols):
        if step == 1 or step % 2 == 0:
            sent(left_ref.at[j], left_send.at[step])
        if step % 2 == 0:
            sent(left_ref.at[j], left_forward.at[step])
    for plane in range(rows):
        for strip in range(per_plane):
            slot = plane * per_plane + strip

            @pl.when((plane <= z) & (z < rows - 1))
            def _(slot=slot):
                sent(right_ref.at[j], up_send.at[slot])

            @pl.when((plane >= z) & (z > 0))
            def _(slot=slot):
                sent(right_ref.at[j], down_send.at[slot])

            @pl.when((plane != z) & (slot != j))
            def _(slot=slot):
                sent(right_ref.at[j], right_send.at[slot])


def gather(rows, cols, width, matrix_real, matrix_imag, indices):
    pairs, depth = matrix_real.shape
    dma = pltpu.SemaphoreType.DMA((cols,))
    return pl.pallas_call(
        functools.partial(gather_kernel, rows, cols),
        out_shape=(
            jax.ShapeDtypeStruct((depth, cols * 2 * pairs), jnp.bfloat16),
            jax.ShapeDtypeStruct((cols, 2 * pairs, width), jnp.bfloat16),
            jax.ShapeDtypeStruct((cols, pairs, 128), jnp.float32),
        ),
        in_specs=[VMEM, VMEM, SMEM, SMEM, SMEM, SMEM],
        out_specs=(VMEM, VMEM, VMEM),
        scratch_shapes=[
            pltpu.VMEM((cols, 2 * pairs, depth), jnp.bfloat16),
            pltpu.VMEM((rows, 2 * pairs, depth), jnp.bfloat16),
        ]
        + [dma] * 10,
        compiler_params=pltpu.CompilerParams(
            collective_id=0, has_side_effects=True, vmem_limit_bytes=60 * 1024 * 1024
        ),
    )(matrix_real, matrix_imag, *indices)


def product_kernel(
    pairs, frequency_ref, gap_ref, right_ref, turned_ref, real_ref, imag_ref, scaled
):
    cols, both, width = right_ref.shape
    index = pl.program_id(1)
    start = pl.program_id(2)

    @pl.when(pl.program_id(0) == 0)
    def _():
        block = real_ref.shape[2]
        columns = pl.ds(pl.multiple_of(start * block, block), block)
        omega = frequency_ref[index]
        for shard in range(cols):
            gap = gap_ref[shard]
            weight = (4.0 * gap / (gap * gap + omega * omega))[:, :1]
            wide_real = right_ref[shard, :pairs, columns].astype(jnp.float32)
            wide_imag = right_ref[shard, pairs:, columns].astype(jnp.float32)
            scaled_real = (weight * wide_real).astype(jnp.bfloat16)
            scaled_imag = (weight * wide_imag).astype(jnp.bfloat16)
            upper = slice(shard * both, shard * both + pairs)
            lower = slice(shard * both + pairs, (shard + 1) * both)
            scaled[2 * index, upper, columns] = -scaled_real
            scaled[2 * index, lower, columns] = -scaled_imag
            scaled[2 * index + 1, upper, columns] = -scaled_imag
            scaled[2 * index + 1, lower, columns] = scaled_real

    block = real_ref.shape[2]
    chunk = 256
    for part, out_ref in ((0, real_ref), (1, imag_ref)):
        for place in range(0, block, chunk):
            columns = pl.ds(pl.multiple_of(start * block + place, chunk), chunk)
            out_ref[0, :, place : place + chunk] = jnp.dot(
                turned_ref[...],
                scaled[2 * index + part, :, columns],
                preferred_element_type=jnp.float32,
            ).astype(out_ref.dtype)


def product(frequency, gap, right, turned):
    cols, both, width = right.shape
    depth = turned.shape[0]
    count = frequency.shape[0]
    tile = 1024
    block = min(width, 1024)
    out = jax.ShapeDtypeStruct((count, depth, width), jnp.bfloat16)
    out_spec = pl.BlockSpec((1, tile, block), lambda i, f, h: (f, i, h))
    return pl.pallas_call(
        functools.partial(product_kernel, both // 2),
        out_shape=(out, out),
        grid=(depth // tile, count, width // block),
        in_specs=[
            SMEM,
            pl.BlockSpec(gap.shape, lambda i, f, h: (0, 0, 0)),
            pl.BlockSpec(right.shape, lambda i, f, h: (0, 0, 0)),
            pl.BlockSpec((tile, cols * both), lambda i, f, h: (i, 0)),
        ],
        out_specs=(out_spec, out_spec),
        scratch_shapes=[
            pltpu.VMEM((2 * count, cols * both, width), jnp.bfloat16),
        ],
        compiler_params=pltpu.CompilerParams(vmem_limit_bytes=60 * 1024 * 1024),
    )(frequency, gap, right, turned)


def solution(mesh):
    rows, cols = mesh.shape["row"], mesh.shape["col"]

    def on_device(matrix_real, matrix_imag, valence_index, conduction_index,
                  valence_energy, conduction_energy, frequency):
        width = matrix_real.shape[1] * rows // cols
        turned, right, gap = gather(
            rows, cols, width, matrix_real, matrix_imag,
            (valence_index, conduction_index, valence_energy, conduction_energy),
        )
        return product(frequency, gap, right, turned)

    placed = (P("col", "row"), P("col", "row"), P("col"), P("col"), P(), P(), P())
    return jax.shard_map(
        on_device,
        mesh=mesh,
        in_specs=placed,
        out_specs=(P(None, "row", "col"), P(None, "row", "col")),
        check_vma=False,
    )
```
